512 devices in a mesh: dp: 8 (over z_hi, core), state: 64 (over y, x, z_lo).
Axes of the slice: x: 4, y: 4, z: 16 (z_hi: 4, z_lo: 4; z = z_hi * 4 + z_lo), core: 2. Of those that a mesh axis runs over, the one named last changes fastest.
Arguments:
- forward_probs: float32 [2, 512, 8192], P(None, 'dp', 'state'), as said below
- backward_last: float32 [512, 8192], P('dp', 'state'), as said below
- emission: float32 [1024, 8192], P(None, 'state'), as said below
- token_ids: int32 [512, 2], P('dp'), may hold values from 0 to 1023
- transition: bfloat16 [8192, 8192], P('state'), as said below
Outputs:
- backward_first: float32 [512, 8192], P('dp', 'state')
- count_ratio: float32 [8192, 8192], P('state', 'dp')
The draws below stay inside these ranges and needn't reach their ends.
Inputs may be any that keep to these rules, and one draw needn't show every extreme that they name: `transition`: positive weights. `emission`: positive. `forward_probs`: positive. `backward_last`: positive.
All inputs are finite; a program needn't handle non-finite values.
Results may differ from the reference program's by a relative error of at most 0.0029.
Values may be sent and summed in bfloat16 or wider, within the bound.
No kernel may reach another device: no remote copies, remote signals or barrier semaphores. Data moves between devices by JAX's collectives and lax.ppermute only.
A program may use at most 64 MiB of HBM per device.

```python
import math
import jax
import jax.numpy as jnp
import numpy as np

H = 8192
K = 1024
STEPS = 2
SEQS = 512


def draw_transition(key, part):
    key = jax.random.fold_in(key, 11)
    base = jnp.clip(jax.random.normal(key, (H, H), jnp.float32), -5.0, 5.0) * 3.5
    return jnp.exp(base - 12.0).astype(jnp.bfloat16)


def draw_emission(key, part):
    key = jax.random.fold_in(key, 23)
    base = jnp.clip(jax.random.normal(key, (K, H), jnp.float32), -5.0, 5.0) * 2.0
    return jnp.exp(base - 1.0)


def draw_forward_probs(key, part):
    key = jax.random.fold_in(key, 37)
    base = jnp.clip(jax.random.normal(key, (STEPS, SEQS, H), jnp.float32), -5.0, 5.0) * 1.5
    return jnp.exp(base)


def draw_backward_last(key, part):
    key = jax.random.fold_in(key, 53)
    base = jnp.clip(jax.random.normal(key, (SEQS, H), jnp.float32), -5.0, 5.0) * 1.5
    return jnp.exp(base)


def touch_ends(result, own_key, smallest, largest):
    extent = result.shape
    spot = [jax.random.randint(jax.random.fold_in(own_key, axis), (), 0, extent[axis]) for axis in range(len(extent))]
    result = result.at[tuple(spot)].set(smallest)
    longest = extent.index(max(extent))
    spot[longest] = (spot[longest] + 1) % extent[longest]
    return result.at[tuple(spot)].set(largest)


def cumulative_ranks(number_of, slope):
    loads = [(1 << 20) // math.isqrt(rank ** slope) + 1 for rank in range(1, number_of + 1)]
    width = 1 + sum(loads) // (1 << 30)
    return np.cumsum(np.array([max(1, weight // width) for weight in loads]))


def skewed_ids(key, shape, amount, slope):
    table = cumulative_ranks(amount, slope)
    ticket = jax.random.randint(jax.random.fold_in(key, 1), shape, 0, int(table[amount - 1]))
    rank = jnp.searchsorted(jnp.asarray(table, jnp.int32), ticket, side="right")
    return jax.random.permutation(jax.random.fold_in(key, 2), amount)[rank].astype(jnp.int32)


def setup_inputs(seed: int = 0) -> dict:
    keys = jax.random.split(jax.random.key(seed), 6)
    return {
        "forward_probs": draw_forward_probs(jax.random.fold_in(keys[5], 71), 0),
        "backward_last": draw_backward_last(jax.random.fold_in(keys[5], 71), 0),
        "emission": draw_emission(jax.random.fold_in(keys[5], 71), 0),
        "token_ids": touch_ends(skewed_ids(keys[3], (SEQS, STEPS), K, 2), jax.random.fold_in(keys[3], 3), 0, K - 1).astype(jnp.int32),
        "transition": draw_transition(jax.random.fold_in(keys[5], 71), 0),
    }


def reference(forward_probs, backward_last, emission, token_ids, transition):
    backward = backward_last
    total = jnp.zeros((H, H), jnp.float32)
    for step in reversed(range(STEPS)):
        emitted = emission[token_ids[:, step]]
        weighted = (emitted * backward).astype(jnp.bfloat16)
        propagated = jnp.dot(weighted, transition.T, preferred_element_type=jnp.float32)
        scale_back = jnp.sum(propagated, axis=1) / H
        scale_post = jnp.sum(forward_probs[step] * propagated, axis=1) / H
        backward = propagated / scale_back[:, None]
        posterior = (forward_probs[step] / scale_post[:, None]).astype(jnp.bfloat16)
        total = total + jnp.dot(posterior.T, weighted, preferred_element_type=jnp.float32)
    return backward, total / (STEPS * SEQS)
```

```python
import jax
import jax.numpy as jnp
from jax import lax
from jax.sharding import Mesh, PartitionSpec as P

SIZES = (4, 2, 4, 2, 2, 4)
AXES = ("zh", "co", "y", "xh", "xl", "zl")
DP = ("zh", "co")
STATE = ("y", "xh", "xl", "zl")
PLANE = ("y", "xh", "xl")
LINE = ("zh", "co", "zl")


def spread(block, axes):
    count = lax.axis_size(axes)
    return lax.all_to_all(
        jnp.broadcast_to(block[None], (count,) + block.shape), axes, 0, 0, tiled=True
    )


def split3(value):
    high = lax.reduce_precision(value, 8, 7)
    middle = lax.reduce_precision(value - high, 8, 7)
    low = value - high - middle
    return jnp.stack([high, middle, low]).astype(jnp.bfloat16)


def swap_groups(block):
    pairs = []
    for source in range(512):
        zl, xl, xh = source % 4, source // 4 % 2, source // 8 % 2
        y, co, zh = source // 16 % 4, source // 64 % 2, source // 128
        pairs.append((source, ((((y * 2 + xh) * 4 + zh) * 2 + co) * 2 + xl) * 4 + zl))
    return lax.ppermute(block, AXES, pairs)


def on_device(forward_probs, backward_last, emission, token_ids, transition):
    rows, width = transition.shape
    seqs = backward_last.shape[0]
    steps = forward_probs.shape[0]
    groups = lax.axis_size(DP)

    forward_all = lax.all_gather(forward_probs, DP)
    emitted = jnp.take(emission, token_ids.T.reshape(-1), axis=0).reshape(steps, seqs, rows)

    weighted = (emitted[1] * backward_last).astype(jnp.bfloat16)
    col_sums = split3(jnp.sum(transition.astype(jnp.float32), axis=0).reshape(-1, rows))
    packed = spread(jnp.concatenate([weighted[None], col_sums]), "zl")
    line1 = packed[:, 0]
    col_line = split3(jnp.sum(packed[:, 1:].astype(jnp.float32), axis=(0, 1)))
    far1 = swap_groups(line1)
    packed = spread(jnp.concatenate([line1, col_line]), PLANE)
    gathered = packed[:, :4].reshape(-1, seqs, rows)
    col_all = jnp.sum(packed[:, 4:].astype(jnp.float32), axis=(0, 1))
    columns1 = lax.all_gather(far1, PLANE)

    trans = transition.reshape(rows, -1, rows)
    prop1 = lax.dot_general(
        gathered, trans, (((0, 2), (1, 2)), ((), ())), preferred_element_type=jnp.float32
    )
    norm = jnp.sum(gathered.astype(jnp.float32) * col_all[:, None, :], axis=(0, 2)) / width
    post1 = jnp.sum(forward_probs[1] * prop1, axis=1)
    weighted = (emitted[0] * (prop1 / norm[:, None])).astype(jnp.bfloat16)

    line0 = spread(weighted, "zl")
    far0 = swap_groups(line0)
    gathered = spread(line0, PLANE).reshape(-1, seqs, rows)
    prop0 = lax.dot_general(
        gathered, trans, (((0, 2), (1, 2)), ((), ())), preferred_element_type=jnp.float32
    )
    sums = jnp.stack([post1, jnp.sum(forward_probs[0] * prop0, axis=1), jnp.sum(prop0, axis=1)])
    columns0 = spread(far0, PLANE)
    sums = jnp.sum(spread(sums, PLANE), axis=0)
    sums = jnp.sum(spread(sums, LINE).reshape(groups, -1, 3, seqs), axis=1) / width
    mine = lax.dynamic_index_in_dim(sums, lax.axis_index(DP), 0, keepdims=False)
    backward = prop0 / mine[2][:, None]
    total = None
    for step, columns, post in ((1, columns1, sums[:, 0]), (0, columns0, sums[:, 1])):
        posterior = (forward_all[:, step] / post[:, :, None]).astype(jnp.bfloat16)
        cols = columns.reshape(groups, -1, seqs, rows)
        term = lax.dot_general(
            posterior, cols, (((0, 1), (0, 2)), ((), ())), preferred_element_type=jnp.float32
        )
        total = term if total is None else total + term
    return (backward, total.reshape(rows, -1) / (steps * groups * seqs))


def solution(mesh):
    fine = Mesh(mesh.devices.reshape(SIZES), AXES)
    placed = (P(None, DP, STATE), P(DP, STATE), P(None, STATE), P(DP, None), P(STATE, None))
    return jax.shard_map(
        on_device,
        mesh=fine,
        in_specs=placed,
        out_specs=(P(DP, STATE), P(STATE, DP)),
        check_vma=False,
    )
```

```python
import functools

import jax
import jax.numpy as jnp
from jax import lax
from jax.experimental import pallas as pl
from jax.experimental.pallas import tpu as pltpu
from jax.sharding import Mesh, PartitionSpec as P

SIZES = (4, 2, 4, 2, 2, 4)
AXES = ("zh", "co", "y", "xh", "xl", "zl")
DP = ("zh", "co")
STATE = ("y", "xh", "xl", "zl")
PLANE = ("y", "xh", "xl")
LINE = ("zh", "co", "zl")
GROUPS, SHARDS, PLANES, LINES = 8, 64, 16, 4
BF, F32 = jnp.bfloat16, jnp.float32


def exchange(blocks, axes):
    return lax.all_to_all(blocks, axes, 0, 0, tiled=True)


def spread(block, axes):
    return exchange(jnp.broadcast_to(block[None], (lax.axis_size(axes),) + block.shape), axes)


def swap_groups(block):
    pairs = []
    for source in range(512):
        zl, xl, xh = source % 4, source // 4 % 2, source // 8 % 2
        y, co, zh = source // 16 % 4, source // 64 % 2, source // 128
        pairs.append((source, ((((y * 2 + xh) * 4 + zh) * 2 + co) * 2 + xl) * 4 + zl))
    return lax.ppermute(block, AXES, pairs)


def call(body, outs, scratch=(), scalars=0, name=None, after=()):
    vmem, smem = pl.BlockSpec(memory_space=pltpu.VMEM), pl.BlockSpec(memory_space=pltpu.SMEM)

    def run(*args):
        def kernel(*refs):
            body(*refs[: len(args)], *refs[len(args) + len(after) :])

        return pl.pallas_call(
            kernel,
            out_shape=[jax.ShapeDtypeStruct(s, d) for s, d in outs],
            in_specs=[smem] * scalars + [vmem] * (len(args) - scalars)
            + [pl.BlockSpec(memory_space=pl.ANY)] * len(after),
            out_specs=[vmem] * len(outs),
            scratch_shapes=[pltpu.VMEM(s, d) for s, d in scratch],
            compiler_params=pltpu.CompilerParams(vmem_limit_bytes=24 << 20),
            name=name,
        )(*args, *after)

    return run


def put_split(ref, at, value):
    rows = value.shape[0]
    for part in range(3):
        piece = value.astype(BF)
        ref[at, part * rows + 64 : (part + 1) * rows + 64, :] = piece
        value = value - piece.astype(F32)


def to_rows(*columns):
    lane = lax.broadcasted_iota(jnp.int32, (64, 128), 1)
    table = jnp.zeros((64, 128), F32)
    for k, column in enumerate(columns):
        table = jnp.where(lane == k, column, table)
    rows = table.T[0:8, :]
    return jnp.concatenate([rows, jnp.zeros((8, 64), F32)], axis=1)


def to_columns(rows):
    return rows.T[0:64, :]


def start_body(emitted, backward, trans, out):
    weighted = (emitted[...] * backward[...]).astype(BF)
    for zl in range(LINES):
        out[zl, 0:64, :] = weighted
        sums = []
        for p in range(PLANES):
            s = p * LINES + zl
            block = trans[:, s * 128 : (s + 1) * 128].astype(F32)
            sums.append(jnp.sum(block, axis=0, keepdims=True))
        put_split(out, zl, jnp.concatenate(sums, axis=0))


def line_body(got, line, out):
    total = jnp.zeros((16, 128), F32)
    for zl in range(LINES):
        for part in range(3):
            total += got[zl, 64 + part * 16 : 80 + part * 16, :].astype(F32)
    pieces = []
    for part in range(3):
        piece = total.astype(BF)
        pieces.append(piece)
        total = total - piece.astype(F32)
    for zl in range(LINES):
        block = got[zl, 0:64, :]
        line[zl * 64 : (zl + 1) * 64, :] = block
        for p in range(PLANES):
            out[p, zl * 64 : (zl + 1) * 64, :] = block
    for p in range(PLANES):
        for part in range(3):
            out[p, 256 + part * 16 : 272 + part * 16, :] = pieces[part]


def propagate(got, trans, wide):
    for s in range(SHARDS):
        zl = s % LINES
        wide[:, s * 128 : (s + 1) * 128] = got[s // LINES, zl * 64 : (zl + 1) * 64, :]
    return lax.dot_general(
        wide[...], trans[...], (((1,), (1,)), ((), ())), preferred_element_type=F32
    )


def first_body(zl, got, trans, emitted, forward, out, post, wide):
    prop = propagate(got, trans, wide)
    sums = jnp.zeros((16, 128), F32)
    for p in range(PLANES):
        for part in range(3):
            sums += got[p, 256 + part * 16 : 272 + part * 16, :].astype(F32)
    scale = jnp.zeros((64, 128), F32)
    own = pl.multiple_of(zl[0] * 64, 64)
    for p in range(PLANES):
        scale += got[p, pl.ds(own, 64), :].astype(F32) * sums[p : p + 1, :]
    scale = jnp.sum(scale, axis=1, keepdims=True)
    peak = jnp.max(prop, axis=1, keepdims=True)
    out[0:64, :] = emitted[...] * (prop / peak)
    out[64:72, :] = to_rows(peak, scale)
    post[...] = jnp.broadcast_to(
        jnp.sum(forward[...] * prop, axis=1, keepdims=True), (64, 128)
    )


def round_body(width, got, line, out):
    infos = [to_columns(got[zl, 64:72, :]) for zl in range(LINES)]
    scale = (infos[0][:, 1:2] + infos[1][:, 1:2] + infos[2][:, 1:2] + infos[3][:, 1:2]) / width
    for zl in range(LINES):
        block = (got[zl, 0:64, :] * (infos[zl][:, 0:1] / scale)).astype(BF)
        line[zl * 64 : (zl + 1) * 64, :] = block
        for p in range(PLANES):
            out[p, zl * 64 : (zl + 1) * 64, :] = block


def second_body(got, trans, forward, post, far, prop_out, out, wide):
    prop = propagate(got, trans, wide)
    prop_out[...] = prop
    rows = to_rows(
        post[:, 0:1],
        jnp.sum(forward[...] * prop, axis=1, keepdims=True),
        jnp.sum(prop, axis=1, keepdims=True),
    )
    pieces = []
    for part in range(3):
        piece = rows.astype(BF)
        pieces.append(piece.astype(F32))
        rows = rows - pieces[-1]
    tail = jnp.concatenate(pieces + [jnp.zeros((8, 128), F32)], axis=0).astype(BF)
    for p in range(PLANES):
        out[p, 0:256, :] = far[...]
        out[p, 256:288, :] = tail


def sum_body(got, out):
    total = jnp.zeros((32, 128), F32)
    for p in range(PLANES):
        total += got[p, 256:288, :].astype(F32)
    total = total[0:8] + total[8:16] + total[16:24]
    for k in range(GROUPS * LINES):
        out[k] = total


def count_body(width, place, got, everyone, prop, late, early, backward, count, left, right):
    zh, co = place[0], place[1]
    own = zh * 2 + co
    mine = to_columns(jnp.sum(got[pl.ds(own * LINES, LINES)], axis=0) / width)
    backward[...] = prop[...] / mine[:, 2:3]
    for k in range(4):
        for c in range(2):
            g = lax.rem(zh + 4 - k, 4) * 2 + (co if c == 0 else 1 - co)
            sums = to_columns(jnp.sum(got[pl.ds(g * LINES, LINES)], axis=0) / width)
            for t, src in enumerate((late, early)):
                at = t * 512 + (k * 2 + c) * 64
                forward = everyone[g, 1 - t]
                left[at : at + 64, :] = (forward / sums[:, t : t + 1]).astype(BF)
                for p in range(2):
                    for zl in range(LINES):
                        shard = p * LINES + zl
                        right[at : at + 64, shard * 128 : (shard + 1) * 128] = src[
                            g * 2 + p, zl * 64 : (zl + 1) * 64, :
                        ]
    count[...] = jnp.dot(left[...].T, right[...], preferred_element_type=F32) * (1.0 / 1024)


def along(block, axis, step):
    size = lax.axis_size(axis)
    return lax.ppermute(block, axis, [(k, (k + step) % size) for k in range(size)])


def on_device(forward_probs, backward_last, emission, token_ids, transition):
    width = transition.shape[1]
    emitted = emission.at[token_ids.T.reshape(-1)].get(mode="promise_in_bounds")
    emitted = emitted.reshape(2, 64, 128)
    wide = [((64, 8192), BF)]

    (sent,) = call(start_body, [((4, 112, 128), BF)], name="start")(
        emitted[1], backward_last, transition
    )
    got = exchange(sent, "zl")
    line1, sent = call(line_body, [((256, 128), BF), ((16, 304, 128), BF)], name="line")(got)
    far1 = swap_groups(line1)
    forward_all = lax.all_gather(jnp.concatenate([forward_probs, forward_probs]), DP)
    got = exchange(sent, PLANE)
    zl = lax.axis_index("zl").reshape(1)
    sent, post1 = call(
        first_body,
        [((72, 128), F32), ((64, 128), F32)],
        wide,
        1,
        name="first",
        after=(far1,),
    )(zl, got, transition, emitted[0], forward_probs[1])
    late = lax.all_gather(far1, PLANE)
    got = spread(sent, "zl")
    line0, sent = call(
        functools.partial(round_body, width), [((256, 128), BF), ((16, 256, 128), BF)], name="round"
    )(got)
    far0 = swap_groups(line0)
    got = exchange(sent, PLANE)
    prop0, sent = call(
        second_body, [((64, 128), F32), ((16, 288, 128), BF)], wide, name="second"
    )(got, transition, forward_probs[0], post1, far0)
    early = exchange(sent, PLANE)
    (sent,) = call(sum_body, [((32, 8, 128), F32)], name="sums")(early)
    got = exchange(sent, LINE)
    place = jnp.stack([lax.axis_index("zh"), lax.axis_index("co")])
    return tuple(
        call(
            functools.partial(count_body, width),
            [((64, 128), F32), ((128, 1024), F32)],
            [((1024, 128), BF), ((1024, 1024), BF)],
            1,
            name="counts",
        )(place, got, forward_all, prop0, late, early)
    )


def solution(mesh):
    fine = Mesh(mesh.devices.reshape(SIZES), AXES)
    placed = (P(None, DP, STATE), P(DP, STATE), P(None, STATE), P(DP, None), P(STATE, None))
    return jax.shard_map(
        on_device,
        mesh=fine,
        in_specs=placed,
        out_specs=(P(DP, STATE), P(STATE, DP)),
        check_vma=False,
    )
```

```python
import functools

import jax
import jax.numpy as jnp
from jax import lax
from jax.experimental import pallas as pl
from jax.experimental.pallas import tpu as pltpu
from jax.sharding import Mesh, PartitionSpec as P

SIZES = (4, 2, 4, 2, 2, 4)
AXES = ("zh", "co", "y", "xh", "xl", "zl")
DP = ("zh", "co")
STATE = ("y", "xh", "xl", "zl")
PLANE = ("y", "xh", "xl")
LINE = ("zh", "co", "zl")
GROUPS, SHARDS, PLANES, LINES = 8, 64, 16, 4
BF, F32 = jnp.bfloat16, jnp.float32


def exchange(blocks, axes):
    return lax.all_to_all(blocks, axes, 0, 0, tiled=True)


def spread(block, axes):
    return exchange(jnp.broadcast_to(block[None], (lax.axis_size(axes),) + block.shape), axes)


def swap_groups(block):
    pairs = []
    for source in range(512):
        zl, xl, xh = source % 4, source // 4 % 2, source // 8 % 2
        y, co, zh = source // 16 % 4, source // 64 % 2, source // 128
        pairs.append((source, ((((y * 2 + xh) * 4 + zh) * 2 + co) * 2 + xl) * 4 + zl))
    return lax.ppermute(block, AXES, pairs)


PLACES = {
    "vmem": pl.BlockSpec(memory_space=pltpu.VMEM),
    "smem": pl.BlockSpec(memory_space=pltpu.SMEM),
    "any": pl.BlockSpec(memory_space=pl.ANY),
    "hbm": pl.BlockSpec(memory_space=pltpu.HBM),
}


def call(name, body, args, outs, scratch=(), after=(), limit=24):
    def kernel(*refs):
        body(*refs[: len(args)], *refs[len(args) + len(after) :])

    return pl.pallas_call(
        kernel,
        out_shape=[jax.ShapeDtypeStruct(s, d) for s, d, _ in outs],
        in_specs=[PLACES[place] for place, _ in args] + [PLACES["any"]] * len(after),
        out_specs=[PLACES[place] for _, _, place in outs],
        scratch_shapes=list(scratch),
        compiler_params=pltpu.CompilerParams(vmem_limit_bytes=limit << 20),
        name=name,
    )(*[array for _, array in args], *after)


def split3(value):
    pieces = []
    for _ in range(3):
        pieces.append(value.astype(BF))
        value = value - pieces[-1].astype(F32)
    return pieces


def to_rows(*columns):
    lane = lax.broadcasted_iota(jnp.int32, (64, 128), 1)
    table = jnp.zeros((64, 128), F32)
    for k, column in enumerate(columns):
        table = jnp.where(lane == k, column, table)
    rows = table.T[0:8, :]
    return jnp.concatenate([rows, jnp.zeros((8, 64), F32)], axis=1)


def to_columns(rows):
    return rows.T[0:64, :]


def start_body(tokens, emission, backward, trans, out, emitted, rows, now, held, sems):
    width = trans.shape[1] // LINES
    copies = [
        pltpu.make_async_copy(emission, rows, sems.at[LINES]),
        pltpu.make_async_copy(backward, now, sems.at[LINES + 1]),
    ]
    for k in range(LINES):
        part = pl.ds(k * width, width)
        copies.append(pltpu.make_async_copy(trans.at[:, part], held.at[:, part], sems.at[k]))
    for copy in copies:
        copy.start()
    copies[0].wait()
    for b in range(64):
        emitted[b : b + 1, :] = rows[pl.ds(tokens[1, b], 1), :]
    copies[1].wait()
    weighted = (emitted[...] * now[...]).astype(BF)
    for b in range(64):
        emitted[b : b + 1, :] = rows[pl.ds(tokens[0, b], 1), :]
    sums = [[] for _ in range(LINES)]
    for k in range(LINES):
        copies[2 + k].wait()
        for s in range(k * 16, k * 16 + 16):
            block = held[:, s * 128 : (s + 1) * 128].astype(F32)
            sums[s % LINES].append(jnp.sum(block, axis=0, keepdims=True))
    for zl in range(LINES):
        out[zl, 0:64, :] = weighted
        for part, piece in enumerate(split3(jnp.concatenate(sums[zl], axis=0))):
            out[zl, 64 + part * 16 : 80 + part * 16, :] = piece


def line_body(got, line, out):
    total = jnp.zeros((16, 128), F32)
    for zl in range(LINES):
        for part in range(3):
            total += got[zl, 64 + part * 16 : 80 + part * 16, :].astype(F32)
    pieces = split3(total)
    for zl in range(LINES):
        block = got[zl, 0:64, :]
        line[zl * 64 : (zl + 1) * 64, :] = block
        for p in range(PLANES):
            out[p, zl * 64 : (zl + 1) * 64, :] = block
    for p in range(PLANES):
        for part in range(3):
            out[p, 256 + part * 16 : 272 + part * 16, :] = pieces[part]


def propagate(got, trans, wide):
    for s in range(SHARDS):
        zl = s % LINES
        wide[:, s * 128 : (s + 1) * 128] = got[s // LINES, zl * 64 : (zl + 1) * 64, :]
    return lax.dot_general(
        wide[...], trans[...], (((1,), (1,)), ((), ())), preferred_element_type=F32
    )


def first_body(zl, got, trans, emitted, forward, out, post, wide):
    prop = propagate(got, trans, wide)
    sums = jnp.zeros((16, 128), F32)
    for p in range(PLANES):
        for part in range(3):
            sums += got[p, 256 + part * 16 : 272 + part * 16, :].astype(F32)
    scale = jnp.zeros((64, 128), F32)
    own = pl.multiple_of(zl[0] * 64, 64)
    for p in range(PLANES):
        scale += got[p, pl.ds(own, 64), :].astype(F32) * sums[p : p + 1, :]
    scale = jnp.sum(scale, axis=1, keepdims=True)
    peak = jnp.max(prop, axis=1, keepdims=True)
    value, info = emitted[...] * (prop / peak), to_rows(peak, scale)
    for k in range(LINES):
        out[k, 0:64, :] = value
        out[k, 64:72, :] = info
    post[...] = jnp.broadcast_to(
        jnp.sum(forward[...] * prop, axis=1, keepdims=True), (64, 128)
    )


def round_body(width, got, far, line, out):
    infos = [to_columns(got[zl, 64:72, :]) for zl in range(LINES)]
    scale = (infos[0][:, 1:2] + infos[1][:, 1:2] + infos[2][:, 1:2] + infos[3][:, 1:2]) / width
    for zl in range(LINES):
        block = (got[zl, 0:64, :] * (infos[zl][:, 0:1] / scale)).astype(BF)
        line[zl * 64 : (zl + 1) * 64, :] = block
        for p in range(PLANES):
            out[p, zl * 64 : (zl + 1) * 64, :] = block
    for p in range(PLANES):
        out[p, 256:512, :] = far[...]


def second_body(got, trans, forward, post, far, prop_out, out, wide):
    prop = propagate(got, trans, wide)
    prop_out[...] = prop
    rows = to_rows(
        post[:, 0:1],
        jnp.sum(forward[...] * prop, axis=1, keepdims=True),
        jnp.sum(prop, axis=1, keepdims=True),
    )
    pieces = [piece.astype(F32) for piece in split3(rows)]
    tail = jnp.concatenate(pieces + [jnp.zeros((8, 128), F32)], axis=0).astype(BF)
    for p in range(PLANES):
        out[p, 0:256, :] = far[...]
        out[p, 256:288, :] = tail


def sum_body(got, out):
    total = jnp.zeros((32, 128), F32)
    for p in range(PLANES):
        total += got[p, 256:288, :].astype(F32)
    total = total[0:8] + total[8:16] + total[16:24]
    both = total[0:1] + pltpu.roll(total[1:2], 64, axis=1)
    pair = jnp.concatenate([both, total[2:3]], axis=0)
    for k in range(GROUPS * LINES):
        out[k] = pair


def prepare_body(late, early, forward, right, held, sems):
    copies = []
    for g in range(GROUPS):
        copies.append(pltpu.make_async_copy(forward.at[g, pl.ds(0, 2)], held.at[g], sems.at[g]))
        copies[-1].start()
    for t, (src, first) in enumerate(((late, 256), (early, 0))):
        for g in range(GROUPS):
            at = t * 512 + g * 64
            for c in range(GROUPS):
                rows = first + c % LINES * 64
                right[at : at + 64, c * 128 : (c + 1) * 128] = src[
                    g * 2 + c // LINES, rows : rows + 64, :
                ]
    for copy in copies:
        copy.wait()


def count_body(width, group, got, forward, prop, right, backward, count, left):
    def columns(first):
        pair = jnp.sum(got[pl.ds(first, LINES)], axis=0) / width
        table = jnp.concatenate([pair, jnp.zeros((6, 128), F32)], axis=0).T
        return table[0:64, 0:1], table[64:128, 0:1], table[0:64, 1:2]

    backward[...] = prop[...] / columns(group[0] * LINES)[2]
    for g in range(GROUPS):
        post = columns(g * LINES)
        for t in range(2):
            at = t * 512 + g * 64
            left[at : at + 64, :] = (forward[g, 1 - t] / post[t]).astype(BF)
    count[...] = jnp.dot(left[...].T, right[...], preferred_element_type=F32) * (1.0 / 1024)


def on_device(forward_probs, backward_last, emission, token_ids, transition):
    width = transition.shape[1]
    wide = pltpu.VMEM((64, 8192), BF)

    forward_all = lax.all_gather(jnp.concatenate([forward_probs, forward_probs]), DP)
    sent, emitted = call(
        "start",
        start_body,
        [("smem", token_ids.T), ("hbm", emission), ("hbm", backward_last), ("hbm", transition)],
        [((4, 112, 128), BF, "vmem"), ((64, 128), F32, "vmem")],
        [
            pltpu.VMEM(emission.shape, F32),
            pltpu.VMEM((64, 128), F32),
            pltpu.VMEM((128, 8192), BF),
            pltpu.SemaphoreType.DMA((LINES + 2,)),
        ],
        limit=60,
    )
    got = exchange(sent, "zl")
    line1, sent = call(
        "line",
        line_body,
        [("vmem", got)],
        [((256, 128), BF, "vmem"), ((16, 304, 128), BF, "vmem")],
    )
    far1 = swap_groups(line1)
    got = exchange(sent, PLANE)
    sent, post1 = call(
        "first",
        first_body,
        [
            ("smem", lax.axis_index("zl").reshape(1)),
            ("vmem", got),
            ("vmem", transition),
            ("vmem", emitted),
            ("vmem", forward_probs[1]),
        ],
        [((4, 72, 128), F32, "vmem"), ((64, 128), F32, "vmem")],
        [wide],
        (far1,),
    )
    got = exchange(sent, "zl")
    line0, sent = call(
        "round",
        functools.partial(round_body, width),
        [("vmem", got), ("vmem", far1)],
        [((256, 128), BF, "vmem"), ((16, 512, 128), BF, "vmem")],
    )
    far0 = swap_groups(line0)
    got = exchange(sent, PLANE)
    prop0, sent = call(
        "second",
        second_body,
        [("vmem", got), ("vmem", transition), ("vmem", forward_probs[0]), ("vmem", post1)]
        + [("vmem", far0)],
        [((64, 128), F32, "vmem"), ((16, 288, 128), BF, "vmem")],
        [wide],
    )
    early = exchange(sent, PLANE)
    (sent,) = call("sums", sum_body, [("vmem", early)], [((32, 2, 128), F32, "vmem")])
    right, forward = call(
        "prepare",
        prepare_body,
        [("vmem", got), ("vmem", early), ("any", forward_all)],
        [((1024, 1024), BF, "vmem"), ((8, 2, 64, 128), F32, "vmem")],
        [pltpu.SemaphoreType.DMA((GROUPS,))],
    )
    got = exchange(sent, LINE)
    group = lax.axis_index(DP).reshape(1)
    return tuple(
        call(
            "counts",
            functools.partial(count_body, width),
            [("smem", group), ("vmem", got), ("vmem", forward), ("vmem", prop0), ("vmem", right)],
            [((64, 128), F32, "vmem"), ((128, 1024), F32, "vmem")],
            [pltpu.VMEM((1024, 128), BF)],
        )
    )


def solution(mesh):
    fine = Mesh(mesh.devices.reshape(SIZES), AXES)
    placed = (P(None, DP, STATE), P(DP, STATE), P(None, STATE), P(DP, None), P(STATE, None))
    return jax.shard_map(
        on_device,
        mesh=fine,
        in_specs=placed,
        out_specs=(P(DP, STATE), P(STATE, DP)),
        check_vma=False,
    )
```

```python
import functools

import jax
import jax.numpy as jnp
from jax import lax
from jax.experimental import pallas as pl
from jax.experimental.pallas import tpu as pltpu
from jax.sharding import Mesh, PartitionSpec as P

SIZES = (4, 2, 4, 2, 2, 4)
AXES = ("zh", "co", "y", "xh", "xl", "zl")
DP = ("zh", "co")
STATE = ("y", "xh", "xl", "zl")
PLANE = ("y", "xh", "xl")
LINE = ("zh", "co", "zl")
GROUPS, SHARDS, PLANES, LINES = 8, 64, 16, 4
BF, F32 = jnp.bfloat16, jnp.float32


def exchange(blocks, axes):
    return lax.all_to_all(blocks, axes, 0, 0, tiled=True)


def spread(block, axes):
    return exchange(jnp.broadcast_to(block[None], (lax.axis_size(axes),) + block.shape), axes)


def swap_groups(block):
    pairs = []
    for source in range(512):
        zl, xl, xh = source % 4, source // 4 % 2, source // 8 % 2
        y, co, zh = source // 16 % 4, source // 64 % 2, source // 128
        pairs.append((source, ((((y * 2 + xh) * 4 + zh) * 2 + co) * 2 + xl) * 4 + zl))
    return lax.ppermute(block, AXES, pairs)


PLACES = {
    "vmem": pl.BlockSpec(memory_space=pltpu.VMEM),
    "smem": pl.BlockSpec(memory_space=pltpu.SMEM),
    "any": pl.BlockSpec(memory_space=pl.ANY),
    "hbm": pl.BlockSpec(memory_space=pltpu.HBM),
}


def call(name, body, args, outs, scratch=(), after=(), limit=24):
    def kernel(*refs):
        body(*refs[: len(args)], *refs[len(args) + len(after) :])

    return pl.pallas_call(
        kernel,
        out_shape=[jax.ShapeDtypeStruct(s, d) for s, d, _ in outs],
        in_specs=[PLACES[place] for place, _ in args] + [PLACES["any"]] * len(after),
        out_specs=[PLACES[place] for _, _, place in outs],
        scratch_shapes=list(scratch),
        compiler_params=pltpu.CompilerParams(vmem_limit_bytes=limit << 20),
        name=name,
    )(*[array for _, array in args], *after)


def split3(value):
    pieces = []
    for _ in range(3):
        pieces.append(value.astype(BF))
        value = value - pieces[-1].astype(F32)
    return pieces


def to_rows(*columns):
    lane = lax.broadcasted_iota(jnp.int32, (64, 128), 1)
    table = jnp.zeros((64, 128), F32)
    for k, column in enumerate(columns):
        table = jnp.where(lane == k, column, table)
    rows = table.T[0:8, :]
    return jnp.concatenate([rows, jnp.zeros((8, 64), F32)], axis=1)


def to_columns(rows):
    return rows.T[0:64, :]


def start_body(tokens, emission, backward, trans, out, emitted, rows, now, held, sems):
    width = trans.shape[1] // LINES
    copies = [
        pltpu.make_async_copy(emission, rows, sems.at[LINES]),
        pltpu.make_async_copy(backward, now, sems.at[LINES + 1]),
    ]
    for k in range(LINES):
        part = pl.ds(k * width, width)
        copies.append(pltpu.make_async_copy(trans.at[:, part], held.at[:, part], sems.at[k]))
    for copy in copies:
        copy.start()
    copies[0].wait()
    for b in range(64):
        emitted[b : b + 1, :] = rows[pl.ds(tokens[1, b], 1), :]
    copies[1].wait()
    weighted = (emitted[...] * now[...]).astype(BF)
    for b in range(64):
        emitted[b : b + 1, :] = rows[pl.ds(tokens[0, b], 1), :]
    sums = [[] for _ in range(LINES)]
    for k in range(LINES):
        copies[2 + k].wait()
        for s in range(k * 16, k * 16 + 16):
            block = held[:, s * 128 : (s + 1) * 128].astype(F32)
            sums[s % LINES].append(jnp.sum(block, axis=0, keepdims=True))
    for zl in range(LINES):
        out[zl, 0:64, :] = weighted
        for part, piece in enumerate(split3(jnp.concatenate(sums[zl], axis=0))):
            out[zl, 64 + part * 16 : 80 + part * 16, :] = piece


def line_body(got, line, out):
    total = jnp.zeros((16, 128), F32)
    for zl in range(LINES):
        for part in range(3):
            total += got[zl, 64 + part * 16 : 80 + part * 16, :].astype(F32)
    pieces = split3(total)
    for zl in range(LINES):
        block = got[zl, 0:64, :]
        line[zl * 64 : (zl + 1) * 64, :] = block
        for p in range(PLANES):
            out[p, zl * 64 : (zl + 1) * 64, :] = block
    for p in range(PLANES):
        for part in range(3):
            out[p, 256 + part * 16 : 272 + part * 16, :] = pieces[part]


def propagate(got, trans, wide):
    for s in range(SHARDS):
        zl = s % LINES
        wide[:, s * 128 : (s + 1) * 128] = got[s // LINES, zl * 64 : (zl + 1) * 64, :]
    return lax.dot_general(
        wide[...], trans[...], (((1,), (1,)), ((), ())), preferred_element_type=F32
    )


def first_body(zl, got, trans, emitted, forward, out, post, wide):
    prop = propagate(got, trans, wide)
    sums = jnp.zeros((16, 128), F32)
    for p in range(PLANES):
        for part in range(3):
            sums += got[p, 256 + part * 16 : 272 + part * 16, :].astype(F32)
    scale = jnp.zeros((64, 128), F32)
    own = pl.multiple_of(zl[0] * 64, 64)
    for p in range(PLANES):
        scale += got[p, pl.ds(own, 64), :].astype(F32) * sums[p : p + 1, :]
    scale = jnp.sum(scale, axis=1, keepdims=True)
    peak = jnp.max(prop, axis=1, keepdims=True)
    value, info = emitted[...] * (prop / peak), to_rows(peak, scale)
    for k in range(LINES):
        out[k, 0:64, :] = value
        out[k, 64:72, :] = info
    post[...] = jnp.broadcast_to(
        jnp.sum(forward[...] * prop, axis=1, keepdims=True), (64, 128)
    )


def round_body(width, got, far, line, out):
    infos = [to_columns(got[zl, 64:72, :]) for zl in range(LINES)]
    scale = (infos[0][:, 1:2] + infos[1][:, 1:2] + infos[2][:, 1:2] + infos[3][:, 1:2]) / width
    for zl in range(LINES):
        block = (got[zl, 0:64, :] * (infos[zl][:, 0:1] / scale)).astype(BF)
        line[zl * 64 : (zl + 1) * 64, :] = block
        for p in range(PLANES):
            out[p, zl * 64 : (zl + 1) * 64, :] = block
    for p in range(PLANES):
        out[p, 256:512, :] = far[...]


def second_body(got, trans, forward, post, far, prop_out, out, wide):
    prop = propagate(got, trans, wide)
    prop_out[...] = prop
    rows = to_rows(
        post[:, 0:1],
        jnp.sum(forward[...] * prop, axis=1, keepdims=True),
        jnp.sum(prop, axis=1, keepdims=True),
    )
    pieces = [piece.astype(F32)[0:4] for piece in split3(rows)]
    tail = jnp.concatenate(pieces + [jnp.zeros((4, 128), F32)], axis=0).astype(BF)
    for p in range(PLANES):
        out[p, 0:256, :] = far[...]
        out[p, 256:272, :] = tail


def sum_body(got, out):
    total = jnp.zeros((16, 128), F32)
    for p in range(PLANES):
        total += got[p, 256:272, :].astype(F32)
    total = total[0:4] + total[4:8] + total[8:12]
    both = total[0:1] + pltpu.roll(total[1:2], 64, axis=1)
    pair = jnp.concatenate([both, total[2:3]], axis=0)
    for k in range(GROUPS * LINES):
        out[k] = pair


def prepare_body(late, early, forward, right1, right0, held, sems):
    copies = []
    for g in range(GROUPS):
        copies.append(pltpu.make_async_copy(forward.at[g, pl.ds(0, 2)], held.at[g], sems.at[g]))
        copies[-1].start()
    for src, first, right in ((late, 256, right1), (early, 0, right0)):
        for g in range(GROUPS):
            at = g * 64
            for c in range(GROUPS):
                rows = first + c % LINES * 64
                right[at : at + 64, c * 128 : (c + 1) * 128] = src[
                    g * 2 + c // LINES, rows : rows + 64, :
                ]
    for copy in copies:
        copy.wait()


def count_body(width, group, got, forward, prop, right1, right0, backward, count, left):
    def columns(first):
        pair = jnp.sum(got[pl.ds(first, LINES)], axis=0) / width
        table = jnp.concatenate([pair, jnp.zeros((6, 128), F32)], axis=0).T
        return table[0:64, 0:1], table[64:128, 0:1], table[0:64, 1:2]

    backward[...] = prop[...] / columns(group[0] * LINES)[2]
    for g in range(GROUPS):
        post = columns(g * LINES)
        for t in range(2):
            at = t * 512 + g * 64
            left[at : at + 64, :] = (forward[g, 1 - t] / post[t]).astype(BF)
    total = jnp.dot(left[0:512, :].T, right1[...], preferred_element_type=F32)
    total += jnp.dot(left[512:1024, :].T, right0[...], preferred_element_type=F32)
    count[...] = total * (1.0 / 1024)


def on_device(forward_probs, backward_last, emission, token_ids, transition):
    width = transition.shape[1]
    wide = pltpu.VMEM((64, 8192), BF)

    forward_all = lax.all_gather(jnp.concatenate([forward_probs, forward_probs]), DP)
    sent, emitted = call(
        "start",
        start_body,
        [("smem", token_ids.T), ("hbm", emission), ("hbm", backward_last), ("hbm", transition)],
        [((4, 112, 128), BF, "vmem"), ((64, 128), F32, "vmem")],
        [
            pltpu.VMEM(emission.shape, F32),
            pltpu.VMEM((64, 128), F32),
            pltpu.VMEM((128, 8192), BF),
            pltpu.SemaphoreType.DMA((LINES + 2,)),
        ],
        limit=60,
    )
    got = exchange(sent, "zl")
    line1, sent = call(
        "line",
        line_body,
        [("vmem", got)],
        [((256, 128), BF, "vmem"), ((16, 304, 128), BF, "vmem")],
    )
    far1 = swap_groups(line1)
    got = exchange(sent, PLANE)
    sent, post1 = call(
        "first",
        first_body,
        [
            ("smem", lax.axis_index("zl").reshape(1)),
            ("vmem", got),
            ("vmem", transition),
            ("vmem", emitted),
            ("vmem", forward_probs[1]),
        ],
        [((4, 72, 128), F32, "vmem"), ((64, 128), F32, "vmem")],
        [wide],
        (far1,),
    )
    got = exchange(sent, "zl")
    line0, sent = call(
        "round",
        functools.partial(round_body, width),
        [("vmem", got), ("vmem", far1)],
        [((256, 128), BF, "vmem"), ((16, 512, 128), BF, "vmem")],
    )
    far0 = swap_groups(line0)
    got = exchange(sent, PLANE)
    prop0, sent = call(
        "second",
        second_body,
        [("vmem", got), ("vmem", transition), ("vmem", forward_probs[0]), ("vmem", post1)]
        + [("vmem", far0)],
        [((64, 128), F32, "vmem"), ((16, 272, 128), BF, "vmem")],
        [wide],
    )
    early = exchange(sent, PLANE)
    (sent,) = call("sums", sum_body, [("vmem", early)], [((32, 2, 128), F32, "vmem")])
    right1, right0, forward = call(
        "prepare",
        prepare_body,
        [("vmem", got), ("vmem", early), ("any", forward_all)],
        [((512, 1024), BF, "vmem")] * 2 + [((8, 2, 64, 128), F32, "vmem")],
        [pltpu.SemaphoreType.DMA((GROUPS,))],
    )
    got = exchange(sent, LINE)
    group = lax.axis_index(DP).reshape(1)
    return tuple(
        call(
            "counts",
            functools.partial(count_body, width),
            [("smem", group), ("vmem", got), ("vmem", forward), ("vmem", prop0)]
            + [("vmem", right1), ("vmem", right0)],
            [((64, 128), F32, "vmem"), ((128, 1024), F32, "vmem")],
            [pltpu.VMEM((1024, 128), BF)],
        )
    )


def solution(mesh):
    fine = Mesh(mesh.devices.reshape(SIZES), AXES)
    placed = (P(None, DP, STATE), P(DP, STATE), P(None, STATE), P(DP, None), P(STATE, None))
    return jax.shard_map(
        on_device,
        mesh=fine,
        in_specs=placed,
        out_specs=(P(DP, STATE), P(STATE, DP)),
        check_vma=False,
    )
```

```python
import functools

import jax
import jax.numpy as jnp
from jax import lax
from jax.experimental import pallas as pl
from jax.experimental.pallas import tpu as pltpu
from jax.sharding import Mesh, PartitionSpec as P

SIZES = (4, 2, 4, 2, 2, 4)
AXES = ("zh", "co", "y", "xh", "xl", "zl")
DP = ("zh", "co")
STATE = ("y", "xh", "xl", "zl")
PLANE = ("y", "xh", "xl")
LINE = ("zh", "co", "zl")
GROUPS, SHARDS, PLANES, LINES = 8, 64, 16, 4
BF, F32 = jnp.bfloat16, jnp.float32


def exchange(blocks, axes):
    return lax.all_to_all(blocks, axes, 0, 0, tiled=True)


def spread(block, axes):
    return exchange(jnp.broadcast_to(block[None], (lax.axis_size(axes),) + block.shape), axes)


def swap_groups(block):
    pairs = []
    for source in range(512):
        zl, xl, xh = source % 4, source // 4 % 2, source // 8 % 2
        y, co, zh = source // 16 % 4, source // 64 % 2, source // 128
        pairs.append((source, ((((y * 2 + xh) * 4 + zh) * 2 + co) * 2 + xl) * 4 + zl))
    return lax.ppermute(block, AXES, pairs)


PLACES = {
    "vmem": pl.BlockSpec(memory_space=pltpu.VMEM),
    "smem": pl.BlockSpec(memory_space=pltpu.SMEM),
    "any": pl.BlockSpec(memory_space=pl.ANY),
    "hbm": pl.BlockSpec(memory_space=pltpu.HBM),
}


def call(name, body, args, outs, scratch=(), after=(), limit=24):
    def kernel(*refs):
        body(*refs[: len(args)], *refs[len(args) + len(after) :])

    return pl.pallas_call(
        kernel,
        out_shape=[jax.ShapeDtypeStruct(s, d) for s, d, _ in outs],
        in_specs=[PLACES[place] for place, _ in args] + [PLACES["any"]] * len(after),
        out_specs=[PLACES[place] for _, _, place in outs],
        scratch_shapes=list(scratch),
        compiler_params=pltpu.CompilerParams(vmem_limit_bytes=limit << 20),
        name=name,
    )(*[array for _, array in args], *after)


def split3(value):
    pieces = []
    for _ in range(3):
        pieces.append(value.astype(BF))
        value = value - pieces[-1].astype(F32)
    return pieces


def to_rows(*columns):
    lane = lax.broadcasted_iota(jnp.int32, (64, 128), 1)
    table = jnp.zeros((64, 128), F32)
    for k, column in enumerate(columns):
        table = jnp.where(lane == k, column, table)
    rows = table.T[0:8, :]
    return jnp.concatenate([rows, jnp.zeros((8, 64), F32)], axis=1)


def to_columns(rows):
    return rows.T[0:64, :]


def start_body(tokens, emission, backward, trans, out, emitted, rows, now, held, sems):
    width = trans.shape[1] // LINES
    copies = [
        pltpu.make_async_copy(emission, rows, sems.at[LINES]),
        pltpu.make_async_copy(backward, now, sems.at[LINES + 1]),
    ]
    for k in range(LINES):
        part = pl.ds(k * width, width)
        copies.append(pltpu.make_async_copy(trans.at[:, part], held.at[:, part], sems.at[k]))
    for copy in copies:
        copy.start()
    copies[0].wait()
    for b in range(64):
        emitted[b : b + 1, :] = rows[pl.ds(tokens[1, b], 1), :]
    copies[1].wait()
    weighted = (emitted[...] * now[...]).astype(BF)
    for b in range(64):
        emitted[b : b + 1, :] = rows[pl.ds(tokens[0, b], 1), :]
    sums = [[] for _ in range(LINES)]
    for k in range(LINES):
        copies[2 + k].wait()
        for s in range(k * 16, k * 16 + 16):
            block = held[:, s * 128 : (s + 1) * 128].astype(F32)
            sums[s % LINES].append(jnp.sum(block, axis=0, keepdims=True))
    for zl in range(LINES):
        out[zl, 0:64, :] = weighted
        for part, piece in enumerate(split3(jnp.concatenate(sums[zl], axis=0))):
            out[zl, 64 + part * 16 : 80 + part * 16, :] = piece


def line_body(got, line, out):
    total = jnp.zeros((16, 128), F32)
    for zl in range(LINES):
        for part in range(3):
            total += got[zl, 64 + part * 16 : 80 + part * 16, :].astype(F32)
    pieces = split3(total)
    for zl in range(LINES):
        block = got[zl, 0:64, :]
        line[zl * 64 : (zl + 1) * 64, :] = block
        for p in range(PLANES):
            out[p, zl * 64 : (zl + 1) * 64, :] = block
    for p in range(PLANES):
        for part in range(3):
            out[p, 256 + part * 16 : 272 + part * 16, :] = pieces[part]


def propagate(got, trans, wide):
    for s in range(SHARDS):
        zl = s % LINES
        wide[:, s * 128 : (s + 1) * 128] = got[s // LINES, zl * 64 : (zl + 1) * 64, :]
    return lax.dot_general(
        wide[...], trans[...], (((1,), (1,)), ((), ())), preferred_element_type=F32
    )


def first_body(zl, got, trans, emitted, forward, out, post, wide):
    prop = propagate(got, trans, wide)
    sums = jnp.zeros((16, 128), F32)
    for p in range(PLANES):
        for part in range(3):
            sums += got[p, 256 + part * 16 : 272 + part * 16, :].astype(F32)
    scale = jnp.zeros((64, 128), F32)
    own = pl.multiple_of(zl[0] * 64, 64)
    for p in range(PLANES):
        scale += got[p, pl.ds(own, 64), :].astype(F32) * sums[p : p + 1, :]
    scale = jnp.sum(scale, axis=1, keepdims=True)
    peak = jnp.max(prop, axis=1, keepdims=True)
    value, info = emitted[...] * (prop / peak), to_rows(peak, scale)
    for k in range(LINES):
        out[k, 0:64, :] = value
        out[k, 64:72, :] = info
    post[...] = jnp.broadcast_to(
        jnp.sum(forward[...] * prop, axis=1, keepdims=True), (64, 128)
    )


def round_body(width, got, far, line, out):
    infos = [to_columns(got[zl, 64:72, :]) for zl in range(LINES)]
    scale = (infos[0][:, 1:2] + infos[1][:, 1:2] + infos[2][:, 1:2] + infos[3][:, 1:2]) / width
    for zl in range(LINES):
        block = (got[zl, 0:64, :] * (infos[zl][:, 0:1] / scale)).astype(BF)
        line[zl * 64 : (zl + 1) * 64, :] = block
        for p in range(PLANES):
            out[p, zl * 64 : (zl + 1) * 64, :] = block
    for p in range(PLANES):
        out[p, 256:512, :] = far[...]


def second_body(got, trans, forward, post, far, prop_out, out, wide, rows, sems):
    copies = []
    for k in range(4):
        part = pl.ds(k * 4, 4)
        copies.append(
            pltpu.make_async_copy(got.at[part, pl.ds(0, 256)], rows.at[part], sems.at[k])
        )
        copies[-1].start()
    for p in range(PLANES):
        out[p, 0:256, :] = far[...]
    for copy in copies:
        copy.wait()
    prop = propagate(rows, trans, wide)
    prop_out[...] = prop
    rows = to_rows(
        post[:, 0:1],
        jnp.sum(forward[...] * prop, axis=1, keepdims=True),
        jnp.sum(prop, axis=1, keepdims=True),
    )
    pieces = [piece.astype(F32)[0:4] for piece in split3(rows)]
    tail = jnp.concatenate(pieces + [jnp.zeros((4, 128), F32)], axis=0).astype(BF)
    for p in range(PLANES):
        out[p, 256:272, :] = tail


def sum_body(got, out):
    total = jnp.zeros((16, 128), F32)
    for p in range(PLANES):
        total += got[p, 256:272, :].astype(F32)
    total = total[0:4] + total[4:8] + total[8:12]
    both = total[0:1] + pltpu.roll(total[1:2], 64, axis=1)
    pair = jnp.concatenate([both, total[2:3]], axis=0)
    for k in range(GROUPS * LINES):
        out[k] = pair


def prepare_body(late, early, forward, right1, right0, held, sems):
    copies = []
    for g in range(GROUPS):
        copies.append(pltpu.make_async_copy(forward.at[g, pl.ds(0, 2)], held.at[g], sems.at[g]))
        copies[-1].start()
    for src, first, right in ((late, 256, right1), (early, 0, right0)):
        for g in range(GROUPS):
            at = g * 64
            for c in range(GROUPS):
                rows = first + c % LINES * 64
                right[at : at + 64, c * 128 : (c + 1) * 128] = src[
                    g * 2 + c // LINES, rows : rows + 64, :
                ]
    for copy in copies:
        copy.wait()


def count_body(width, group, got, forward, prop, right1, right0, backward, count, left):
    def columns(first):
        pair = jnp.sum(got[pl.ds(first, LINES)], axis=0) / width
        table = jnp.concatenate([pair, jnp.zeros((6, 128), F32)], axis=0).T
        return table[0:64, 0:1], table[64:128, 0:1], table[0:64, 1:2]

    backward[...] = prop[...] / columns(group[0] * LINES)[2]
    for g in range(GROUPS):
        post = columns(g * LINES)
        for t in range(2):
            at = t * 512 + g * 64
            left[at : at + 64, :] = (forward[g, 1 - t] / post[t]).astype(BF)
    total = jnp.dot(left[0:512, :].T, right1[...], preferred_element_type=F32)
    total += jnp.dot(left[512:1024, :].T, right0[...], preferred_element_type=F32)
    count[...] = total * (1.0 / 1024)


def on_device(forward_probs, backward_last, emission, token_ids, transition):
    width = transition.shape[1]
    wide = pltpu.VMEM((64, 8192), BF)

    forward_all = lax.all_gather(jnp.concatenate([forward_probs, forward_probs]), DP)
    sent, emitted = call(
        "start",
        start_body,
        [("smem", token_ids.T), ("hbm", emission), ("hbm", backward_last), ("hbm", transition)],
        [((4, 112, 128), BF, "vmem"), ((64, 128), F32, "vmem")],
        [
            pltpu.VMEM(emission.shape, F32),
            pltpu.VMEM((64, 128), F32),
            pltpu.VMEM((128, 8192), BF),
            pltpu.SemaphoreType.DMA((LINES + 2,)),
        ],
        limit=60,
    )
    got = exchange(sent, "zl")
    line1, sent = call(
        "line",
        line_body,
        [("vmem", got)],
        [((256, 128), BF, "vmem"), ((16, 304, 128), BF, "vmem")],
    )
    far1 = swap_groups(line1)
    got = exchange(sent, PLANE)
    sent, post1 = call(
        "first",
        first_body,
        [
            ("smem", lax.axis_index("zl").reshape(1)),
            ("vmem", got),
            ("vmem", transition),
            ("vmem", emitted),
            ("vmem", forward_probs[1]),
        ],
        [((4, 72, 128), F32, "vmem"), ((64, 128), F32, "vmem")],
        [wide],
        (far1,),
    )
    got = exchange(sent, "zl")
    line0, sent = call(
        "round",
        functools.partial(round_body, width),
        [("vmem", got), ("vmem", far1)],
        [((256, 128), BF, "vmem"), ((16, 512, 128), BF, "vmem")],
    )
    far0 = swap_groups(line0)
    got = exchange(sent, PLANE)
    prop0, sent = call(
        "second",
        second_body,
        [("any", got), ("vmem", transition), ("vmem", forward_probs[0]), ("vmem", post1)]
        + [("vmem", far0)],
        [((64, 128), F32, "vmem"), ((16, 272, 128), BF, "vmem")],
        [wide, pltpu.VMEM((16, 256, 128), BF), pltpu.SemaphoreType.DMA((4,))],
    )
    early = exchange(sent, PLANE)
    (sent,) = call("sums", sum_body, [("vmem", early)], [((32, 2, 128), F32, "vmem")])
    right1, right0, forward = call(
        "prepare",
        prepare_body,
        [("vmem", got), ("vmem", early), ("any", forward_all)],
        [((512, 1024), BF, "vmem")] * 2 + [((8, 2, 64, 128), F32, "vmem")],
        [pltpu.SemaphoreType.DMA((GROUPS,))],
    )
    got = exchange(sent, LINE)
    group = lax.axis_index(DP).reshape(1)
    return tuple(
        call(
            "counts",
            functools.partial(count_body, width),
            [("smem", group), ("vmem", got), ("vmem", forward), ("vmem", prop0)]
            + [("vmem", right1), ("vmem", right0)],
            [((64, 128), F32, "vmem"), ((128, 1024), F32, "vmem")],
            [pltpu.VMEM((1024, 128), BF)],
        )
    )


def solution(mesh):
    fine = Mesh(mesh.devices.reshape(SIZES), AXES)
    placed = (P(None, DP, STATE), P(DP, STATE), P(None, STATE), P(DP, None), P(STATE, None))
    return jax.shard_map(
        on_device,
        mesh=fine,
        in_specs=placed,
        out_specs=(P(DP, STATE), P(STATE, DP)),
        check_vma=False,
    )
```

```python
import functools

import jax
import jax.numpy as jnp
from jax import lax
from jax.experimental import pallas as pl
from jax.experimental.pallas import tpu as pltpu
from jax.sharding import Mesh, PartitionSpec as P

SIZES = (4, 2, 4, 2, 2, 4)
AXES = ("zh", "co", "y", "xh", "xl", "zl")
DP = ("zh", "co")
STATE = ("y", "xh", "xl", "zl")
PLANE = ("y", "xh", "xl")
LINE = ("zh", "co", "zl")
GROUPS, SHARDS, PLANES, LINES = 8, 64, 16, 4
BF, F32 = jnp.bfloat16, jnp.float32


def exchange(blocks, axes):
    return lax.all_to_all(blocks, axes, 0, 0, tiled=True)


def spread(block, axes):
    return exchange(jnp.broadcast_to(block[None], (lax.axis_size(axes),) + block.shape), axes)


def swap_groups(block):
    pairs = []
    for source in range(512):
        zl, xl, xh = source % 4, source // 4 % 2, source // 8 % 2
        y, co, zh = source // 16 % 4, source // 64 % 2, source // 128
        pairs.append((source, ((((y * 2 + xh) * 4 + zh) * 2 + co) * 2 + xl) * 4 + zl))
    return lax.ppermute(block, AXES, pairs)


PLACES = {
    "vmem": pl.BlockSpec(memory_space=pltpu.VMEM),
    "smem": pl.BlockSpec(memory_space=pltpu.SMEM),
    "any": pl.BlockSpec(memory_space=pl.ANY),
    "hbm": pl.BlockSpec(memory_space=pltpu.HBM),
}


def call(name, body, args, outs, scratch=(), after=(), limit=24):
    def kernel(*refs):
        body(*refs[: len(args)], *refs[len(args) + len(after) :])

    return pl.pallas_call(
        kernel,
        out_shape=[jax.ShapeDtypeStruct(s, d) for s, d, _ in outs],
        in_specs=[PLACES[place] for place, _ in args] + [PLACES["any"]] * len(after),
        out_specs=[PLACES[place] for _, _, place in outs],
        scratch_shapes=list(scratch),
        compiler_params=pltpu.CompilerParams(vmem_limit_bytes=limit << 20),
        name=name,
    )(*[array for _, array in args], *after)


def split3(value):
    pieces = []
    for _ in range(3):
        pieces.append(value.astype(BF))
        value = value - pieces[-1].astype(F32)
    return pieces


def to_rows(*columns):
    lane = lax.broadcasted_iota(jnp.int32, (64, 128), 1)
    table = jnp.zeros((64, 128), F32)
    for k, column in enumerate(columns):
        table = jnp.where(lane == k, column, table)
    rows = table.T[0:8, :]
    return jnp.concatenate([rows, jnp.zeros((8, 64), F32)], axis=1)


def to_columns(rows):
    return rows.T[0:64, :]


def start_body(tokens, emission, backward, trans, out, emitted, rows, now, held, sems):
    width = trans.shape[1] // LINES
    copies = [
        pltpu.make_async_copy(emission, rows, sems.at[LINES]),
        pltpu.make_async_copy(backward, now, sems.at[LINES + 1]),
    ]
    for k in range(LINES):
        part = pl.ds(k * width, width)
        copies.append(pltpu.make_async_copy(trans.at[:, part], held.at[:, part], sems.at[k]))
    for copy in copies:
        copy.start()
    copies[0].wait()
    for b in range(64):
        emitted[b : b + 1, :] = rows[pl.ds(tokens[1, b], 1), :]
    copies[1].wait()
    weighted = (emitted[...] * now[...]).astype(BF)
    for b in range(64):
        emitted[b : b + 1, :] = rows[pl.ds(tokens[0, b], 1), :]
    sums = [[] for _ in range(LINES)]
    for k in range(LINES):
        copies[2 + k].wait()
        for s in range(k * 16, k * 16 + 16):
            block = held[:, s * 128 : (s + 1) * 128].astype(F32)
            sums[s % LINES].append(jnp.sum(block, axis=0, keepdims=True))
    for zl in range(LINES):
        out[zl, 0:64, :] = weighted
        for part, piece in enumerate(split3(jnp.concatenate(sums[zl], axis=0))):
            out[zl, 64 + part * 16 : 80 + part * 16, :] = piece


def line_body(got, line, out):
    total = jnp.zeros((16, 128), F32)
    for zl in range(LINES):
        for part in range(3):
            total += got[zl, 64 + part * 16 : 80 + part * 16, :].astype(F32)
    pieces = split3(total)
    for zl in range(LINES):
        block = got[zl, 0:64, :]
        line[zl * 64 : (zl + 1) * 64, :] = block
        for p in range(PLANES):
            out[p, zl * 64 : (zl + 1) * 64, :] = block
    for p in range(PLANES):
        for part in range(3):
            out[p, 256 + part * 16 : 272 + part * 16, :] = pieces[part]


def propagate(got, trans, wide):
    for s in range(SHARDS):
        zl = s % LINES
        wide[:, s * 128 : (s + 1) * 128] = got[s // LINES, zl * 64 : (zl + 1) * 64, :]
    return lax.dot_general(
        wide[...], trans[...], (((1,), (1,)), ((), ())), preferred_element_type=F32
    )


def first_body(zl, got, trans, emitted, forward, out, post, wide):
    prop = propagate(got, trans, wide)
    sums = jnp.zeros((16, 128), F32)
    for p in range(PLANES):
        for part in range(3):
            sums += got[p, 256 + part * 16 : 272 + part * 16, :].astype(F32)
    scale = jnp.zeros((64, 128), F32)
    own = pl.multiple_of(zl[0] * 64, 64)
    for p in range(PLANES):
        scale += got[p, pl.ds(own, 64), :].astype(F32) * sums[p : p + 1, :]
    scale = jnp.sum(scale, axis=1, keepdims=True)
    peak = jnp.max(prop, axis=1, keepdims=True)
    out[0:64, :] = emitted[...] * (prop / peak)
    out[64:72, :] = to_rows(peak, scale)
    post[...] = jnp.broadcast_to(
        jnp.sum(forward[...] * prop, axis=1, keepdims=True), (64, 128)
    )


def repeat_body(got, out):
    for k in range(LINES):
        out[k] = got[...]


def round_body(width, got, far, line, out):
    infos = [to_columns(got[zl, 64:72, :]) for zl in range(LINES)]
    scale = (infos[0][:, 1:2] + infos[1][:, 1:2] + infos[2][:, 1:2] + infos[3][:, 1:2]) / width
    for zl in range(LINES):
        block = (got[zl, 0:64, :] * (infos[zl][:, 0:1] / scale)).astype(BF)
        line[zl * 64 : (zl + 1) * 64, :] = block
        for p in range(PLANES):
            out[p, zl * 64 : (zl + 1) * 64, :] = block
    for p in range(PLANES):
        out[p, 256:512, :] = far[...]


def second_body(got, trans, forward, post, far, prop_out, out, wide, rows, sems):
    copies = []
    for k in range(4):
        part = pl.ds(k * 4, 4)
        copies.append(
            pltpu.make_async_copy(got.at[part, pl.ds(0, 256)], rows.at[part], sems.at[k])
        )
        copies[-1].start()
    for p in range(PLANES):
        out[p, 0:256, :] = far[...]
    for copy in copies:
        copy.wait()
    prop = propagate(rows, trans, wide)
    prop_out[...] = prop
    rows = to_rows(
        post[:, 0:1],
        jnp.sum(forward[...] * prop, axis=1, keepdims=True),
        jnp.sum(prop, axis=1, keepdims=True),
    )
    pieces = [piece.astype(F32)[0:4] for piece in split3(rows)]
    tail = jnp.concatenate(pieces + [jnp.zeros((4, 128), F32)], axis=0).astype(BF)
    for p in range(PLANES):
        out[p, 256:272, :] = tail


def sum_body(got, out):
    total = jnp.zeros((16, 128), F32)
    for p in range(PLANES):
        total += got[p, 256:272, :].astype(F32)
    total = total[0:4] + total[4:8] + total[8:12]
    both = total[0:1] + pltpu.roll(total[1:2], 64, axis=1)
    pair = jnp.concatenate([both, total[2:3]], axis=0)
    for k in range(GROUPS * LINES):
        out[k] = pair


def prepare_body(late, early, forward, right1, right0, held, sems):
    copies = []
    for g in range(GROUPS):
        copies.append(pltpu.make_async_copy(forward.at[g, pl.ds(0, 2)], held.at[g], sems.at[g]))
        copies[-1].start()
    for src, first, right in ((late, 256, right1), (early, 0, right0)):
        for g in range(GROUPS):
            at = g * 64
            for c in range(GROUPS):
                rows = first + c % LINES * 64
                right[at : at + 64, c * 128 : (c + 1) * 128] = src[
                    g * 2 + c // LINES, rows : rows + 64, :
                ]
    for copy in copies:
        copy.wait()


def count_body(width, group, got, forward, prop, right1, right0, backward, count, left):
    def columns(first):
        pair = jnp.sum(got[pl.ds(first, LINES)], axis=0) / width
        table = jnp.concatenate([pair, jnp.zeros((6, 128), F32)], axis=0).T
        return table[0:64, 0:1], table[64:128, 0:1], table[0:64, 1:2]

    backward[...] = prop[...] / columns(group[0] * LINES)[2]
    for g in range(GROUPS):
        post = columns(g * LINES)
        for t in range(2):
            at = t * 512 + g * 64
            left[at : at + 64, :] = (forward[g, 1 - t] / post[t]).astype(BF)
    total = jnp.dot(left[0:512, :].T, right1[...], preferred_element_type=F32)
    total += jnp.dot(left[512:1024, :].T, right0[...], preferred_element_type=F32)
    count[...] = total * (1.0 / 1024)


def on_device(forward_probs, backward_last, emission, token_ids, transition):
    width = transition.shape[1]
    wide = pltpu.VMEM((64, 8192), BF)

    forward_all = lax.all_gather(jnp.concatenate([forward_probs, forward_probs]), DP)
    sent, emitted = call(
        "start",
        start_body,
        [("smem", token_ids.T), ("hbm", emission), ("hbm", backward_last), ("hbm", transition)],
        [((4, 112, 128), BF, "vmem"), ((64, 128), F32, "vmem")],
        [
            pltpu.VMEM(emission.shape, F32),
            pltpu.VMEM((64, 128), F32),
            pltpu.VMEM((128, 8192), BF),
            pltpu.SemaphoreType.DMA((LINES + 2,)),
        ],
        limit=60,
    )
    got = exchange(sent, "zl")
    line1, sent = call(
        "line",
        line_body,
        [("vmem", got)],
        [((256, 128), BF, "vmem"), ((16, 304, 128), BF, "vmem")],
    )
    far1 = swap_groups(line1)
    got = exchange(sent, PLANE)
    sent, post1 = call(
        "first",
        first_body,
        [
            ("smem", lax.axis_index("zl").reshape(1)),
            ("vmem", got),
            ("vmem", transition),
            ("vmem", emitted),
            ("vmem", forward_probs[1]),
        ],
        [((72, 128), F32, "vmem"), ((64, 128), F32, "vmem")],
        [wide],
    )
    (sent,) = call(
        "repeat",
        repeat_body,
        [("vmem", sent)],
        [((4, 72, 128), F32, "vmem")],
        (),
        (far1,),
    )
    got = exchange(sent, "zl")
    line0, sent = call(
        "round",
        functools.partial(round_body, width),
        [("vmem", got), ("vmem", far1)],
        [((256, 128), BF, "vmem"), ((16, 512, 128), BF, "vmem")],
    )
    far0 = swap_groups(line0)
    got = exchange(sent, PLANE)
    prop0, sent = call(
        "second",
        second_body,
        [("any", got), ("vmem", transition), ("vmem", forward_probs[0]), ("vmem", post1)]
        + [("vmem", far0)],
        [((64, 128), F32, "vmem"), ((16, 272, 128), BF, "vmem")],
        [wide, pltpu.VMEM((16, 256, 128), BF), pltpu.SemaphoreType.DMA((4,))],
    )
    early = exchange(sent, PLANE)
    (sent,) = call("sums", sum_body, [("vmem", early)], [((32, 2, 128), F32, "vmem")])
    right1, right0, forward = call(
        "prepare",
        prepare_body,
        [("vmem", got), ("vmem", early), ("any", forward_all)],
        [((512, 1024), BF, "vmem")] * 2 + [((8, 2, 64, 128), F32, "vmem")],
        [pltpu.SemaphoreType.DMA((GROUPS,))],
    )
    got = exchange(sent, LINE)
    group = lax.axis_index(DP).reshape(1)
    return tuple(
        call(
            "counts",
            functools.partial(count_body, width),
            [("smem", group), ("vmem", got), ("vmem", forward), ("vmem", prop0)]
            + [("vmem", right1), ("vmem", right0)],
            [((64, 128), F32, "vmem"), ((128, 1024), F32, "vmem")],
            [pltpu.VMEM((1024, 128), BF)],
        )
    )


def solution(mesh):
    fine = Mesh(mesh.devices.reshape(SIZES), AXES)
    placed = (P(None, DP, STATE), P(DP, STATE), P(None, STATE), P(DP, None), P(STATE, None))
    return jax.shard_map(
        on_device,
        mesh=fine,
        in_specs=placed,
        out_specs=(P(DP, STATE), P(STATE, DP)),
        check_vma=False,
    )
```
